1024 devices in a mesh: dp: 32 (over z_lo, y), owner: 32 (over x, z_hi, core).
Axes of the slice: x: 4, y: 4, z: 32 (z_hi: 4, z_lo: 8; z = z_hi * 8 + z_lo), core: 2. Of those that a mesh axis runs over, the one named last changes fastest.
Arguments:
- activations: bfloat16 [65536, 512], P('dp'), may hold values from -6 to 6
- cotangent: bfloat16 [32, 512, 65536], P(None, 'owner', 'dp'), may hold values from -0.046875 to 0.046875
- left_basis: float32 [32, 512, 512], P('dp'), may hold values from -1 to 1, as said below
- right_basis: float32 [32, 512, 512], P('dp'), may hold values from -1 to 1, as said below
- first_moment: float32 [32, 512, 512], P('dp', None, 'owner'), may hold values from -4 to 4
- second_moment: float32 [32, 512, 512], P('dp', None, 'owner'), may hold values from 0.01 to 1
- master_weight: float32 [32, 512, 512], P('dp', 'owner'), may hold values from -0.3125 to 0.3125
Outputs:
- new_weight: float32 [32, 512, 512], P('dp', 'owner')
- compute_weight: bfloat16 [32, 512, 512], P('dp', 'owner')
- new_first: float32 [32, 512, 512], P('dp', None, 'owner')
- new_second: float32 [32, 512, 512], P('dp', None, 'owner')
The draws below stay inside these ranges and needn't reach their ends.
Inputs may be any that keep to these rules, and one draw needn't show every extreme that they name: Each block of left_basis is an orthogonal matrix. Each block of right_basis is an orthogonal matrix.
All inputs are finite; a program needn't handle non-finite values.
Results may differ from the reference program's by a relative error of at most 0.0013.
Values sent between devices are 32-bit elements; how exact they have to be, the bound alone decides.
No kernel may reach another device: no remote copies, remote signals or barrier semaphores. Data moves between devices by JAX's collectives and lax.ppermute only.
A program may use at most 32 MiB of HBM per device.

```python
import math
import jax
import jax.numpy as jnp
from jax import lax

BLOCK = 512
BLOCKS = 32
TOKENS = 65536


def orthogonal_blocks(key):
    order_key, sign_key, angle_key = jax.random.split(key, 3)
    order_keys = jax.random.split(order_key, BLOCKS)
    orders = jax.vmap(lambda one_key: jax.random.permutation(one_key, BLOCK))(order_keys).astype(jnp.int32)
    rows = jnp.arange(BLOCK, dtype=jnp.int32)
    product = (2 * rows[None, :, None] + 1) * (2 * orders[:, None, :] + 1)
    reduced = product % (8 * BLOCK)
    angle = reduced.astype(jnp.float32) * (jnp.pi / (4.0 * BLOCK))
    cosine = jnp.cos(angle) * jnp.sqrt(2.0 / BLOCK)
    signs = (2 * jax.random.randint(sign_key, (BLOCKS, BLOCK, 1), 0, 2) - 1).astype(jnp.float32)
    signed = cosine * signs
    turns = jax.random.uniform(angle_key, (BLOCKS, BLOCK // 2, 1), jnp.float32, -jnp.pi, jnp.pi)
    paired = signed.reshape(BLOCKS, BLOCK // 2, 2, BLOCK)
    upper = paired[:, :, 0, :]
    lower = paired[:, :, 1, :]
    turn_cos = jnp.cos(turns)
    turn_sin = jnp.sin(turns)
    new_upper = turn_cos * upper - turn_sin * lower
    new_lower = turn_sin * upper + turn_cos * lower
    return jnp.stack([new_upper, new_lower], axis=2).reshape(BLOCKS, BLOCK, BLOCK)


def draw_left_basis(key, part):
    key = jax.random.fold_in(key, 11)
    return orthogonal_blocks(key)


def draw_right_basis(key, part):
    key = jax.random.fold_in(key, 23)
    return orthogonal_blocks(key)


def strengthened(drawn, rng, source, target, shards_of, factor):
    owner, partner = [(jnp.arange(drawn.shape[axis_at]) // (drawn.shape[axis_at] // shards_of)).reshape([-1 if axis == axis_at else 1 for axis in range(drawn.ndim)]) for axis_at in (source, target)]
    chosen = jax.random.permutation(rng, shards_of)[partner]
    strong = (owner == chosen) | (owner == (partner + shards_of // 2) % shards_of)
    return jnp.where(strong, factor * drawn, drawn)


def level_of(own_key, dims, pieces, smallest, top_value):
    factor_of, own = 1.0, jax.random.fold_in(own_key, 6)
    for position, blocks in pieces:
        draws = jnp.exp(jax.random.uniform(jax.random.fold_in(own, position), (blocks,), jnp.float32, smallest / len(pieces), top_value / len(pieces)))
        factor_of = factor_of * jnp.repeat(draws, dims[position] // blocks).reshape([-1 if axis == position else 1 for axis in range(len(dims))])
    return factor_of


def bell_draw(stream_key, shape, width, limit, cuts=(), held_as=jnp.bfloat16):
    result = jax.random.normal(stream_key, shape, jnp.float32) * width
    if len(cuts) > 0:
        result = level_of(stream_key, shape, cuts, -0.22, 0.18) * result
    return jnp.clip(result, min=-limit, max=limit).astype(held_as)


def bell_draw_with(stream_key, extent, width, limit, cuts, heavy, kind=jnp.bfloat16):
    drawn = width * jax.random.normal(stream_key, extent, jnp.float32)
    if cuts:
        drawn = drawn * level_of(stream_key, extent, cuts, -0.22, 0.18)
    return jnp.clip(strengthened(drawn, jax.random.fold_in(stream_key, 3), *heavy), -limit, limit).astype(kind)


def setup_inputs(seed: int = 0) -> dict:
    splits = jax.random.split(jax.random.key(seed), 8)
    activations = bell_draw(splits[0], (TOKENS, BLOCK), 1.0, 6.0, ((0, 32),))
    cotangent = bell_draw_with(splits[1], (BLOCKS, BLOCK, TOKENS), TOKENS ** -0.5, 0.046875, ((1, 32), (2, 32)), (2, 0, 32, 2.75))
    left_basis = draw_left_basis(jax.random.fold_in(splits[7], 71), 0)
    right_basis = draw_right_basis(jax.random.fold_in(splits[7], 71), 0)
    first_moment = bell_draw(splits[4], (BLOCKS, BLOCK, BLOCK), 0.3, 4.0, ((0, 32), (2, 32)), jnp.float32)
    second_moment = jnp.clip(jnp.exp(math.log(1.0) - 4.6051702 * jax.random.uniform(splits[5], (BLOCKS, BLOCK, BLOCK), jnp.float32) ** level_of(splits[5], (BLOCKS, BLOCK, BLOCK), ((0, 32), (2, 32)), -0.2, 0.2)), 0.01, 1.0)
    master_weight = bell_draw(splits[6], (BLOCKS, BLOCK, BLOCK), 0.02, 0.3125, ((0, 32), (1, 32)), jnp.float32)
    return dict(activations=activations, cotangent=cotangent, left_basis=left_basis, right_basis=right_basis, first_moment=first_moment, second_moment=second_moment, master_weight=master_weight)


beta_one = 0.9
beta_two = 0.95
correct_one = 1.0 - 0.9 ** 10
correct_two = 1.0 - 0.95 ** 10
epsilon = 1e-08
learning_rate = 0.01

def reference(activations, cotangent, left_basis, right_basis, first_moment, second_moment, master_weight):
    highest = lax.Precision.HIGHEST

    def one_block(block_items):
        cotangent_block, left_matrix, right_matrix, first_block, second_block, weight_block = block_items
        gradient = jnp.dot(cotangent_block, activations, preferred_element_type=jnp.float32)
        rotated = jnp.dot(jnp.dot(left_matrix.T, gradient, precision=highest), right_matrix, precision=highest)
        first_new = beta_one * first_block + (1.0 - beta_one) * rotated
        second_new = beta_two * second_block + (1.0 - beta_two) * rotated * rotated
        direction = first_new / correct_one / (jnp.sqrt(second_new / correct_two) + epsilon)
        update = jnp.dot(jnp.dot(left_matrix, direction, precision=highest), right_matrix.T, precision=highest)
        return (weight_block - learning_rate * update, first_new, second_new)
    new_weight, new_first, new_second = lax.map(one_block, (cotangent, left_basis, right_basis, first_moment, second_moment, master_weight))
    compute_weight = new_weight.astype(jnp.bfloat16)
    return (new_weight, compute_weight, new_first, new_second)
```

```python
import jax
import jax.numpy as jnp
from jax import lax
from jax.sharding import PartitionSpec as P

beta_one = 0.9
beta_two = 0.95
correct_one = 1.0 - 0.9**10
correct_two = 1.0 - 0.95**10
epsilon = 1e-08
learning_rate = 0.01

near_groups = [[(2 * q + p) * 4 + y for p in range(2) for y in range(4)] for q in range(4)]
quad_groups = [[(2 * q + p) * 4 + y for q in range(4)] for p in range(2) for y in range(4)]


def swap_strips(value):
    rows, columns = value.shape
    owners = columns // rows
    packed = value.reshape(rows, owners, rows).transpose(1, 0, 2).reshape(owners, 2, rows * rows // 2)
    packed = lax.all_to_all(packed, "owner", 0, 0, tiled=True)
    return packed.reshape(owners, rows, rows).transpose(2, 0, 1).reshape(rows, columns)


def shards(
    activations, cotangent, left_basis, right_basis, first_moment, second_moment, master_weight
):
    precision = lax.Precision.HIGH
    left_matrix = left_basis[0]
    right_matrix = right_basis[0]
    partial = jnp.einsum("bwt,tr->bwr", cotangent, activations, preferred_element_type=jnp.float32)
    partial = partial.reshape(4, 8, 16, 512)
    near = lax.all_to_all(partial, "dp", 1, 1, axis_index_groups=near_groups, tiled=True).sum(1)
    far = lax.all_to_all(near, "dp", 0, 0, axis_index_groups=quad_groups, tiled=True)
    gradient_rows = far.sum(0)
    turned = swap_strips(jnp.dot(gradient_rows, right_matrix, precision=precision))
    rotated = jnp.dot(turned, left_matrix, precision=precision)
    first_new = beta_one * first_moment[0].T + (1.0 - beta_one) * rotated
    second_new = beta_two * second_moment[0].T + (1.0 - beta_two) * rotated * rotated
    direction = first_new / correct_one / (jnp.sqrt(second_new / correct_two) + epsilon)
    half = swap_strips(jnp.einsum("cj,ij->ci", direction, left_matrix, precision=precision))
    update = jnp.einsum("ik,jk->ij", half, right_matrix, precision=precision)
    weight_new = master_weight[0] - learning_rate * update
    rounded_weight = weight_new.astype(jnp.bfloat16)
    return (weight_new[None], rounded_weight[None], first_new.T[None], second_new.T[None])


def solution(mesh):
    in_specs = (
        P("dp", None),
        P(None, "owner", "dp"),
        P("dp", None, None),
        P("dp", None, None),
        P("dp", None, "owner"),
        P("dp", None, "owner"),
        P("dp", "owner", None),
    )
    out_specs = (
        P("dp", "owner", None),
        P("dp", "owner", None),
        P("dp", None, "owner"),
        P("dp", None, "owner"),
    )
    return jax.shard_map(shards, mesh=mesh, in_specs=in_specs, out_specs=out_specs, check_vma=False)
```

```python
import jax
import jax.numpy as jnp
from jax import lax
from jax.sharding import PartitionSpec as P

beta_one = 0.9
beta_two = 0.95
correct_one = 1.0 - 0.9**10
correct_two = 1.0 - 0.95**10
epsilon = 1e-08
learning_rate = 0.01

near_groups = [[(2 * q + p) * 4 + y for p in range(2) for y in range(4)] for q in range(4)]
quad_groups = [[(2 * q + p) * 4 + y for q in (2, 3, 0, 1)] for p in range(2) for y in range(4)]

owner_order = [(x * 4 + h) * 2 + c for x in range(4) for h in (2, 3, 0, 1) for c in range(2)]


def swap_strips(value):
    rows, columns = value.shape
    owners = columns // rows
    packed = value.reshape(rows, owners, rows).transpose(1, 0, 2).reshape(owners, 2, rows * rows // 2)
    packed = jnp.roll(packed.reshape(4, 4, -1, 128), 2, 1).reshape(owners, 2, 128)
    packed = lax.all_to_all(packed, "owner", 0, 0, axis_index_groups=[owner_order], tiled=True)
    packed = jnp.roll(packed.reshape(4, 4, -1, 128), 2, 1)
    return packed.reshape(owners, rows, rows).transpose(2, 0, 1).reshape(rows, columns)


def shards(
    activations, cotangent, left_basis, right_basis, first_moment, second_moment, master_weight
):
    precision = lax.Precision.HIGH
    left_matrix = left_basis[0]
    right_matrix = right_basis[0]
    partial = jnp.einsum("bwt,tr->bwr", cotangent, activations, preferred_element_type=jnp.float32)
    partial = partial.reshape(4, 8, 16, 512)
    near = lax.all_to_all(partial, "dp", 1, 1, axis_index_groups=near_groups, tiled=True).sum(1)
    near = jnp.roll(near, 2, 0)
    far = lax.all_to_all(near, "dp", 0, 0, axis_index_groups=quad_groups, tiled=True)
    gradient_rows = far.sum(0)
    turned = swap_strips(jnp.dot(gradient_rows, right_matrix, precision=precision))
    rotated = jnp.dot(turned, left_matrix, precision=precision)
    first_new = beta_one * first_moment[0].T + (1.0 - beta_one) * rotated
    second_new = beta_two * second_moment[0].T + (1.0 - beta_two) * rotated * rotated
    direction = first_new / correct_one / (jnp.sqrt(second_new / correct_two) + epsilon)
    half = swap_strips(jnp.einsum("cj,ij->ci", direction, left_matrix, precision=precision))
    update = jnp.einsum("ik,jk->ij", half, right_matrix, precision=precision)
    weight_new = master_weight[0] - learning_rate * update
    rounded_weight = weight_new.astype(jnp.bfloat16)
    return (weight_new[None], rounded_weight[None], first_new.T[None], second_new.T[None])


def solution(mesh):
    in_specs = (
        P("dp", None),
        P(None, "owner", "dp"),
        P("dp", None, None),
        P("dp", None, None),
        P("dp", None, "owner"),
        P("dp", None, "owner"),
        P("dp", "owner", None),
    )
    out_specs = (
        P("dp", "owner", None),
        P("dp", "owner", None),
        P("dp", None, "owner"),
        P("dp", None, "owner"),
    )
    return jax.shard_map(shards, mesh=mesh, in_specs=in_specs, out_specs=out_specs, check_vma=False)
```

```python
import jax
import jax.numpy as jnp
from jax import lax
from jax.experimental import pallas as pl
from jax.experimental.pallas import tpu as pltpu
from jax.sharding import PartitionSpec as P

beta_one = 0.9
beta_two = 0.95
correct_one = 1.0 - 0.9**10
correct_two = 1.0 - 0.95**10
epsilon = 1e-08
learning_rate = 0.01

near_groups = [[(2 * q + p) * 4 + y for p in range(2) for y in range(4)] for q in range(4)]
quad_groups = [[(2 * q + p) * 4 + y for q in (2, 3, 0, 1)] for p in range(2) for y in range(4)]

owner_order = [(x * 4 + h) * 2 + c for x in range(4) for h in (2, 3, 0, 1) for c in range(2)]


def split(value):
    high = value.astype(jnp.bfloat16)
    return high, (value - high.astype(jnp.float32)).astype(jnp.bfloat16)


def product(left, right, contract):
    left_high, left_low = split(left)
    right_high, right_low = split(right)

    def one(x, y):
        return lax.dot_general(
            x, y, (((1,), (contract,)), ((), ())), preferred_element_type=jnp.float32
        )

    return one(left_high, right_low) + one(left_low, right_high) + one(left_high, right_high)


def pack_strips(value, tall, packed):
    tall[:, :16] = value.T
    lane = lax.broadcasted_iota(jnp.int32, (64, 128), 1) // 16
    total = jnp.zeros((64, 128), jnp.float32)
    for t in range(8):
        row = tall[pl.ds(t, 64, stride=8), :]
        if t:
            row = pltpu.roll(row, 16 * t, 1)
        total = jnp.where(lane == t, row, total)
    for tile in range(8):
        other = tile ^ 1
        packed[8 * other : 8 * other + 8, :] = total[8 * tile : 8 * tile + 8]


def unpack_strips(packed, wide):
    lane = lax.broadcasted_iota(jnp.int32, (8, 128), 1) // 16
    row = lax.broadcasted_iota(jnp.int32, (8, 128), 0)
    for half in range(2):
        for x in range(4):
            block = packed[pl.ds(16 * x + half, 8, stride=2), :]
            for step in (4, 2, 1):
                in_row = (row & step) != 0
                in_lane = (lane & step) != 0
                down = pltpu.roll(pltpu.roll(block, step, 0), 128 - 16 * step, 1)
                up = pltpu.roll(pltpu.roll(block, 8 - step, 0), 16 * step, 1)
                moved = jnp.where(in_row, down, up)
                block = jnp.where(in_row == in_lane, block, moved)
            wide[8 * half : 8 * half + 8, 128 * x : 128 * x + 128] = pltpu.roll(block, 64, 1)


def turn_kernel(far, right, packed, tall):
    rows = (far[0] + far[1]) + (far[2] + far[3])
    pack_strips(product(rows, right[...], 0), tall, packed)


def step_kernel(received, left, first, second, packed, first_out, second_out, tall, wide):
    unpack_strips(received, wide)
    rotated = product(wide[...], left[...], 0)
    first_new = beta_one * first[...] + (1.0 - beta_one) * rotated
    second_new = beta_two * second[...] + (1.0 - beta_two) * rotated * rotated
    first_out[...] = first_new
    second_out[...] = second_new
    direction = first_new / correct_one / (jnp.sqrt(second_new / correct_two) + epsilon)
    pack_strips(product(direction, left[...], 1), tall, packed)


def weight_kernel(received, right, weight, weight_out, rounded_out, wide):
    unpack_strips(received, wide)
    weight_new = weight[...] - learning_rate * product(wide[...], right[...], 1)
    weight_out[...] = weight_new
    rounded_out[...] = weight_new.astype(jnp.bfloat16)


def call(kernel, outs, scratch, flops, *args):
    moved = sum(x.size * x.dtype.itemsize for x in (*args, *outs))
    return pl.pallas_call(
        kernel,
        out_shape=outs,
        in_specs=[pl.BlockSpec(memory_space=pltpu.VMEM)] * len(args),
        out_specs=[pl.BlockSpec(memory_space=pltpu.VMEM)] * len(outs),
        scratch_shapes=[pltpu.VMEM(shape, jnp.float32) for shape in scratch],
        cost_estimate=pl.CostEstimate(flops=flops, bytes_accessed=moved, transcendentals=0),
        compiler_params=pltpu.CompilerParams(vmem_limit_bytes=16 * 2**20),
    )(*args)


def exchange(packed):
    swapped = lax.all_to_all(
        packed.reshape(32, 2, 128), "owner", 0, 0, axis_index_groups=[owner_order], tiled=True
    )
    return swapped.reshape(64, 128)


def shards(
    activations, cotangent, left_basis, right_basis, first_moment, second_moment, master_weight
):
    left_matrix = left_basis[0]
    right_matrix = right_basis[0]
    partial = jnp.einsum("bwt,tr->bwr", cotangent, activations, preferred_element_type=jnp.float32)
    partial = partial.reshape(4, 8, 16, 512)
    near = lax.all_to_all(partial, "dp", 1, 1, axis_index_groups=near_groups, tiled=True).sum(1)
    near = jnp.roll(near, 2, 0)
    far = lax.all_to_all(near, "dp", 0, 0, axis_index_groups=quad_groups, tiled=True)
    strip = jax.ShapeDtypeStruct((16, 512), jnp.float32)
    rounded = jax.ShapeDtypeStruct((16, 512), jnp.bfloat16)
    parcel = jax.ShapeDtypeStruct((64, 128), jnp.float32)
    tall, wide = (512, 128), (16, 512)
    work = 6 * 16 * 512 * 512
    (packed,) = call(turn_kernel, [parcel], [tall], work, far, right_matrix)
    packed, first_new, second_new = call(
        step_kernel,
        [parcel, strip, strip],
        [tall, wide],
        2 * work,
        exchange(packed),
        left_matrix,
        first_moment[0].T,
        second_moment[0].T,
    )
    weight_new, weight_rounded = call(
        weight_kernel, [strip, rounded], [wide], work, exchange(packed), right_matrix, master_weight[0]
    )
    return (weight_new[None], weight_rounded[None], first_new.T[None], second_new.T[None])


def solution(mesh):
    in_specs = (
        P("dp", None),
        P(None, "owner", "dp"),
        P("dp", None, None),
        P("dp", None, None),
        P("dp", None, "owner"),
        P("dp", None, "owner"),
        P("dp", "owner", None),
    )
    out_specs = (
        P("dp", "owner", None),
        P("dp", "owner", None),
        P("dp", None, "owner"),
        P("dp", None, "owner"),
    )
    return jax.shard_map(shards, mesh=mesh, in_specs=in_specs, out_specs=out_specs, check_vma=False)
```

```python
import jax
import jax.numpy as jnp
from jax import lax
from jax.experimental import pallas as pl
from jax.experimental.pallas import tpu as pltpu
from jax.sharding import PartitionSpec as P

beta_one = 0.9
beta_two = 0.95
correct_one = 1.0 - 0.9**10
correct_two = 1.0 - 0.95**10
epsilon = 1e-08
learning_rate = 0.01

near_groups = [[8 * q + m for m in range(8)] for q in range(4)]
far_groups = [[8 * q + m for q in (2, 3, 0, 1)] for m in range(8)]
owner_order = [(x * 4 + h) * 2 + c for x in range(4) for h in (2, 3, 0, 1) for c in range(2)]


def split(value):
    high = value.astype(jnp.bfloat16)
    return high, (value - high.astype(jnp.float32)).astype(jnp.bfloat16)


def dot(left, right, contract):
    return lax.dot_general(
        left, right, (((1,), (contract,)), ((), ())), preferred_element_type=jnp.float32
    )


def product(left, right, contract):
    high, low = split(left)
    right_high, right_low = split(right)
    main = dot(jnp.concatenate([high, low], 0), right_high, contract)
    return (dot(high, right_low, contract) + main[16:]) + main[:16]


def product_turned(left, right):
    left_high, left_low = split(left)
    high, low = split(right)
    main = dot(left_high, jnp.concatenate([high, low], 0), 1)
    return (dot(left_low, high, 1) + main[:, 16:]) + main[:, :16]


def pack_strips(value, tall, packed):
    tall[:, :16] = value
    lane = lax.broadcasted_iota(jnp.int32, (64, 128), 1) // 16
    total = jnp.zeros((64, 128), jnp.float32)
    for t in range(8):
        row = tall[pl.ds(t, 64, stride=8), :]
        if t:
            row = pltpu.roll(row, 16 * t, 1)
        total = jnp.where(lane == t, row, total)
    for tile in range(8):
        other = tile ^ 1
        packed[8 * other : 8 * other + 8, :] = total[8 * tile : 8 * tile + 8]


def unpack_strips(packed, wide):
    lane = lax.broadcasted_iota(jnp.int32, (8, 128), 1) // 16
    row = lax.broadcasted_iota(jnp.int32, (8, 128), 0)
    for half in range(2):
        for x in range(4):
            block = packed[pl.ds(16 * x + half, 8, stride=2), :]
            for step in (4, 2, 1):
                in_row = (row & step) != 0
                in_lane = (lane & step) != 0
                down = pltpu.roll(pltpu.roll(block, step, 0), 128 - 16 * step, 1)
                up = pltpu.roll(pltpu.roll(block, 8 - step, 0), 16 * step, 1)
                moved = jnp.where(in_row, down, up)
                block = jnp.where(in_row == in_lane, block, moved)
            wide[8 * half : 8 * half + 8, 128 * x : 128 * x + 128] = pltpu.roll(block, 64, 1)


def total_of(terms):
    while len(terms) > 1:
        terms = [x + y for x, y in zip(terms[::2], terms[1::2])]
    return terms[0]


def gradient_kernel(cotangent, activations, partial, cotangent_in, activations_in, arrived):
    near, far = partial.shape[0], partial.shape[1] // 16
    slices, blocks, _, tokens = cotangent_in.shape
    copies = []
    for k in range(slices):
        span = pl.ds(k * tokens, tokens)
        pairs = [(activations.at[span], activations_in.at[k])]
        for part in range(1):
            some = pl.ds(part * blocks // 1, blocks // 1)
            pairs.append((cotangent.at[some, :, span], cotangent_in.at[k, some]))
        copies.append(
            [pltpu.make_async_copy(x, y, arrived.at[k, i]) for i, (x, y) in enumerate(pairs)]
        )
        for copy in copies[-1]:
            copy.start()
    for k in range(slices):
        for copy in copies[k]:
            copy.wait()
        rows = [cotangent_in[k, f * near + n] for n in range(near) for f in range(far)]
        value = jnp.dot(
            jnp.concatenate(rows, 0), activations_in[k], preferred_element_type=jnp.float32
        ).reshape(partial.shape)
        if k:
            partial[...] += value
        else:
            partial[...] = value


def gradient_partial(cotangent, activations, near):
    blocks, rows, tokens = cotangent.shape
    columns = activations.shape[1]
    slices = 4
    share = tokens // slices
    return pl.pallas_call(
        gradient_kernel,
        out_shape=jax.ShapeDtypeStruct((near, blocks // near * rows, columns), jnp.float32),
        in_specs=[pl.BlockSpec(memory_space=pl.ANY)] * 2,
        out_specs=pl.BlockSpec(memory_space=pltpu.VMEM),
        scratch_shapes=[
            pltpu.VMEM((slices, blocks, rows, share), cotangent.dtype),
            pltpu.VMEM((slices, share, columns), activations.dtype),
            pltpu.SemaphoreType.DMA((slices, 1 + 1)),
        ],
        cost_estimate=pl.CostEstimate(
            flops=2 * blocks * rows * tokens * columns, bytes_accessed=5 * 2**20, transcendentals=0
        ),
        compiler_params=pltpu.CompilerParams(vmem_limit_bytes=56 * 2**20),
    )(cotangent, activations)


def sum_kernel(near, summed):
    far = summed.shape[0]
    for f in range(far):
        terms = [near[n, 16 * f : 16 * f + 16, :] for n in range(near.shape[0])]
        summed[(f + far // 2) % far] = total_of(terms)


def turn_kernel(far, right, packed, tall):
    rows = total_of([far[f] for f in range(far.shape[0])])
    pack_strips(product(rows, right[...], 0).T, tall, packed)


def step_kernel(received, left, first, second, packed, first_out, second_out, tall, wide):
    unpack_strips(received, wide)
    rotated = product(wide[...], left[...], 0)
    first_new = beta_one * first[...] + (1.0 - beta_one) * rotated
    second_new = beta_two * second[...] + (1.0 - beta_two) * rotated * rotated
    first_out[...] = first_new
    second_out[...] = second_new
    direction = first_new / correct_one / (jnp.sqrt(second_new / correct_two) + epsilon)
    pack_strips(product_turned(left[...], direction), tall, packed)


def weight_kernel(received, right, weight, weight_out, rounded_out, wide):
    unpack_strips(received, wide)
    weight_new = weight[...] - learning_rate * product(wide[...], right[...], 1)
    weight_out[...] = weight_new
    rounded_out[...] = weight_new.astype(jnp.bfloat16)


def call(kernel, outs, scratch, flops, *args):
    moved = sum(x.size * x.dtype.itemsize for x in (*args, *outs))
    return pl.pallas_call(
        kernel,
        out_shape=outs,
        in_specs=[pl.BlockSpec(memory_space=pltpu.VMEM)] * len(args),
        out_specs=[pl.BlockSpec(memory_space=pltpu.VMEM)] * len(outs),
        scratch_shapes=[pltpu.VMEM(shape, jnp.float32) for shape in scratch],
        cost_estimate=pl.CostEstimate(flops=flops, bytes_accessed=moved, transcendentals=0),
        compiler_params=pltpu.CompilerParams(vmem_limit_bytes=16 * 2**20),
    )(*args)


def exchange(packed):
    swapped = lax.all_to_all(
        packed.reshape(32, 2, 128), "owner", 0, 0, axis_index_groups=[owner_order], tiled=True
    )
    return swapped.reshape(64, 128)


def shards(
    activations, cotangent, left_basis, right_basis, first_moment, second_moment, master_weight
):
    left_matrix = left_basis[0]
    right_matrix = right_basis[0]
    partial = gradient_partial(cotangent, activations, 8)
    near = lax.all_to_all(partial, "dp", 0, 0, axis_index_groups=near_groups, tiled=True)
    summed = jax.ShapeDtypeStruct((4, 16, 512), jnp.float32)
    (near,) = call(sum_kernel, [summed], [], near.size, near)
    far = lax.all_to_all(near, "dp", 0, 0, axis_index_groups=far_groups, tiled=True)
    strip = jax.ShapeDtypeStruct((16, 512), jnp.float32)
    rounded = jax.ShapeDtypeStruct((16, 512), jnp.bfloat16)
    parcel = jax.ShapeDtypeStruct((64, 128), jnp.float32)
    tall, wide = (512, 128), (16, 512)
    work = 6 * 16 * 512 * 512
    (packed,) = call(turn_kernel, [parcel], [tall], work, far, right_matrix)
    packed, first_new, second_new = call(
        step_kernel,
        [parcel, strip, strip],
        [tall, wide],
        2 * work,
        exchange(packed),
        left_matrix,
        first_moment[0].T,
        second_moment[0].T,
    )
    weight_new, weight_rounded = call(
        weight_kernel, [strip, rounded], [wide], work, exchange(packed), right_matrix, master_weight[0]
    )
    return (weight_new[None], weight_rounded[None], first_new.T[None], second_new.T[None])


def solution(mesh):
    in_specs = (
        P("dp", None),
        P(None, "owner", "dp"),
        P("dp", None, None),
        P("dp", None, None),
        P("dp", None, "owner"),
        P("dp", None, "owner"),
        P("dp", "owner", None),
    )
    out_specs = (
        P("dp", "owner", None),
        P("dp", "owner", None),
        P("dp", None, "owner"),
        P("dp", None, "owner"),
    )
    return jax.shard_map(shards, mesh=mesh, in_specs=in_specs, out_specs=out_specs, check_vma=False)
```

```python
import jax
import jax.numpy as jnp
from jax import lax
from jax.experimental import pallas as pl
from jax.experimental.pallas import tpu as pltpu
from jax.sharding import PartitionSpec as P

beta_one = 0.9
beta_two = 0.95
correct_one = 1.0 - 0.9**10
correct_two = 1.0 - 0.95**10
epsilon = 1e-08
learning_rate = 0.01

near_groups = [[8 * q + m for m in range(8)] for q in range(4)]
far_groups = [[8 * q + m for q in (2, 3, 0, 1)] for m in range(8)]
layer_order = (2, 0, 1, 3)
owner_order = [(x * 4 + h) * 2 + c for h in layer_order for x in range(4) for c in range(2)]


def split(value):
    high = value.astype(jnp.bfloat16)
    return high, (value - high.astype(jnp.float32)).astype(jnp.bfloat16)


def dot(left, right, contract):
    return lax.dot_general(
        left, right, (((1,), (contract,)), ((), ())), preferred_element_type=jnp.float32
    )


def product(left, right, contract):
    high, low = split(left)
    right_high, right_low = split(right)
    main = dot(jnp.concatenate([high, low], 0), right_high, contract)
    return (dot(high, right_low, contract) + main[16:]) + main[:16]


def product_turned(left, right):
    left_high, left_low = split(left)
    high, low = split(right)
    main = dot(left_high, jnp.concatenate([high, low], 0), 1)
    return (dot(left_low, high, 1) + main[:, 16:]) + main[:, :16]


def pack_strips(value, tall, packed):
    tall[:, :16] = value
    lane = lax.broadcasted_iota(jnp.int32, (64, 128), 1) // 16
    total = jnp.zeros((64, 128), jnp.float32)
    for t in range(8):
        row = tall[pl.ds(t, 64, stride=8), :]
        if t:
            row = pltpu.roll(row, 16 * t, 1)
        total = jnp.where(lane == t, row, total)
    for spot, layer in enumerate(layer_order):
        for x in range(4):
            here, there = 16 * spot + 4 * x, 16 * x + 4 * layer
            packed[here : here + 4, :] = total[there : there + 4]


def unpack_strips(packed, ordered, wide):
    lane = lax.broadcasted_iota(jnp.int32, (8, 128), 1) // 16
    row = lax.broadcasted_iota(jnp.int32, (8, 128), 0)
    for spot, layer in enumerate(layer_order):
        for x in range(4):
            here, there = 16 * spot + 4 * x, 16 * x + 4 * layer
            ordered[there : there + 4, :] = packed[here : here + 4, :]
    for half in range(2):
        for x in range(4):
            block = ordered[pl.ds(16 * x + half, 8, stride=2), :]
            for step in (4, 2, 1):
                in_row = (row & step) != 0
                in_lane = (lane & step) != 0
                down = pltpu.roll(pltpu.roll(block, step, 0), 128 - 16 * step, 1)
                up = pltpu.roll(pltpu.roll(block, 8 - step, 0), 16 * step, 1)
                moved = jnp.where(in_row, down, up)
                block = jnp.where(in_row == in_lane, block, moved)
            wide[8 * half : 8 * half + 8, 128 * x : 128 * x + 128] = block


def total_of(terms):
    while len(terms) > 1:
        terms = [x + y for x, y in zip(terms[::2], terms[1::2])]
    return terms[0]


def gradient_kernel(cotangent, activations, partial, cotangent_in, activations_in, arrived):
    near, far = partial.shape[0], partial.shape[1] // 16
    slices, blocks, _, tokens = cotangent_in.shape
    copies = []
    for k in range(slices):
        span = pl.ds(k * tokens, tokens)
        pairs = [(activations.at[span], activations_in.at[k])]
        for part in range(1):
            some = pl.ds(part * blocks // 1, blocks // 1)
            pairs.append((cotangent.at[some, :, span], cotangent_in.at[k, some]))
        copies.append(
            [pltpu.make_async_copy(x, y, arrived.at[k, i]) for i, (x, y) in enumerate(pairs)]
        )
        for copy in copies[-1]:
            copy.start()
    for k in range(slices):
        for copy in copies[k]:
            copy.wait()
        rows = [cotangent_in[k, f * near + n] for n in range(near) for f in range(far)]
        value = jnp.dot(
            jnp.concatenate(rows, 0), activations_in[k], preferred_element_type=jnp.float32
        ).reshape(partial.shape)
        if k:
            partial[...] += value
        else:
            partial[...] = value


def gradient_partial(cotangent, activations, near):
    blocks, rows, tokens = cotangent.shape
    columns = activations.shape[1]
    slices = 4
    share = tokens // slices
    return pl.pallas_call(
        gradient_kernel,
        out_shape=jax.ShapeDtypeStruct((near, blocks // near * rows, columns), jnp.float32),
        in_specs=[pl.BlockSpec(memory_space=pl.ANY)] * 2,
        out_specs=pl.BlockSpec(memory_space=pltpu.VMEM),
        scratch_shapes=[
            pltpu.VMEM((slices, blocks, rows, share), cotangent.dtype),
            pltpu.VMEM((slices, share, columns), activations.dtype),
            pltpu.SemaphoreType.DMA((slices, 1 + 1)),
        ],
        cost_estimate=pl.CostEstimate(
            flops=2 * blocks * rows * tokens * columns, bytes_accessed=5 * 2**20, transcendentals=0
        ),
        compiler_params=pltpu.CompilerParams(vmem_limit_bytes=56 * 2**20),
    )(cotangent, activations)


def sum_kernel(near, summed):
    far = summed.shape[0]
    for f in range(far):
        terms = [near[n, 16 * f : 16 * f + 16, :] for n in range(near.shape[0])]
        summed[(f + far // 2) % far] = total_of(terms)


def turn_kernel(far, right, packed, tall):
    rows = total_of([far[f] for f in range(far.shape[0])])
    pack_strips(product(rows, right[...], 0).T, tall, packed)


def step_kernel(received, left, first, second, packed, first_out, second_out, tall, ordered, wide):
    unpack_strips(received, ordered, wide)
    rotated = product(wide[...], left[...], 0)
    first_new = beta_one * first[...] + (1.0 - beta_one) * rotated
    second_new = beta_two * second[...] + (1.0 - beta_two) * rotated * rotated
    first_out[...] = first_new
    second_out[...] = second_new
    direction = first_new / correct_one / (jnp.sqrt(second_new / correct_two) + epsilon)
    pack_strips(product_turned(left[...], direction), tall, packed)


def weight_kernel(received, right, weight, weight_out, rounded_out, ordered, wide):
    unpack_strips(received, ordered, wide)
    weight_new = weight[...] - learning_rate * product(wide[...], right[...], 1)
    weight_out[...] = weight_new
    rounded_out[...] = weight_new.astype(jnp.bfloat16)


def call(kernel, outs, scratch, flops, *args):
    moved = sum(x.size * x.dtype.itemsize for x in (*args, *outs))
    return pl.pallas_call(
        kernel,
        out_shape=outs,
        in_specs=[pl.BlockSpec(memory_space=pltpu.VMEM)] * len(args),
        out_specs=[pl.BlockSpec(memory_space=pltpu.VMEM)] * len(outs),
        scratch_shapes=[pltpu.VMEM(shape, jnp.float32) for shape in scratch],
        cost_estimate=pl.CostEstimate(flops=flops, bytes_accessed=moved, transcendentals=0),
        compiler_params=pltpu.CompilerParams(vmem_limit_bytes=16 * 2**20),
    )(*args)


def exchange(packed):
    swapped = lax.all_to_all(
        packed.reshape(32, 2, 128), "owner", 0, 0, axis_index_groups=[owner_order], tiled=True
    )
    return swapped.reshape(64, 128)


def shards(
    activations, cotangent, left_basis, right_basis, first_moment, second_moment, master_weight
):
    left_matrix = left_basis[0]
    right_matrix = right_basis[0]
    partial = gradient_partial(cotangent, activations, 8)
    near = lax.all_to_all(partial, "dp", 0, 0, axis_index_groups=near_groups, tiled=True)
    summed = jax.ShapeDtypeStruct((4, 16, 512), jnp.float32)
    (near,) = call(sum_kernel, [summed], [], near.size, near)
    far = lax.all_to_all(near, "dp", 0, 0, axis_index_groups=far_groups, tiled=True)
    strip = jax.ShapeDtypeStruct((16, 512), jnp.float32)
    rounded = jax.ShapeDtypeStruct((16, 512), jnp.bfloat16)
    parcel = jax.ShapeDtypeStruct((64, 128), jnp.float32)
    tall, wide = (512, 128), (16, 512)
    work = 6 * 16 * 512 * 512
    (packed,) = call(turn_kernel, [parcel], [tall], work, far, right_matrix)
    packed, first_new, second_new = call(
        step_kernel,
        [parcel, strip, strip],
        [tall, (64, 128), wide],
        2 * work,
        exchange(packed),
        left_matrix,
        first_moment[0].T,
        second_moment[0].T,
    )
    weight_new, weight_rounded = call(
        weight_kernel, [strip, rounded], [(64, 128), wide], work, exchange(packed), right_matrix, master_weight[0]
    )
    return (weight_new[None], weight_rounded[None], first_new.T[None], second_new.T[None])


def solution(mesh):
    in_specs = (
        P("dp", None),
        P(None, "owner", "dp"),
        P("dp", None, None),
        P("dp", None, None),
        P("dp", None, "owner"),
        P("dp", None, "owner"),
        P("dp", "owner", None),
    )
    out_specs = (
        P("dp", "owner", None),
        P("dp", "owner", None),
        P("dp", None, "owner"),
        P("dp", None, "owner"),
    )
    return jax.shard_map(shards, mesh=mesh, in_specs=in_specs, out_specs=out_specs, check_vma=False)
```
